512 devices in a mesh: role: 4 (over x_hi, core), seq: 128 (over z, y, x_lo).
Axes of the slice: x: 4 (x_hi: 2, x_lo: 2; x = x_hi * 2 + x_lo), y: 8, z: 8, core: 2. Of those that a mesh axis runs over, the one named last changes fastest.
Arguments:
- hidden: bfloat16 [16384, 5120], P('seq', 'role'), may hold values from -6 to 6
- gain: float32 [5120], P('role'), may hold values from 0.25 to 1.75
- head_weight: bfloat16 [5120, 64], P('role'), may hold values from -0.078125 to 0.078125
- noise: bfloat16 [16384, 64], P('seq'), may hold values from -6 to 6
- timestep: int32 [1], replicated, may hold values from 100 to 899
- frames: int32 [16384], replicated, may hold values from 0 to 255, never falling along the last dimension, each value on 1 to 128 neighbouring positions
- score_weights: bfloat16 [4, 4, 64, 5120], P('role'), may hold values from -2 to 2
Outputs:
- latent: bfloat16 [16384, 64], P('seq')
- hidden_grad: bfloat16 [16384, 5120], P('seq', 'role')
- head_grad: float32 [5120, 64], P(('role', 'seq'))
- gain_grad: float32 [5120], P(('role', 'seq'))
The draws below stay inside these ranges and needn't reach their ends.
Inputs may be any that keep to these rules, and one draw needn't show every extreme that they name: `frames`: frame numbers never fall; every frame block has 1 to 128 tokens and one has exactly 128.
All inputs are finite; a program needn't handle non-finite values.
Results may differ from the reference program's by a relative error of at most 0.04.
Values may be sent and summed in bfloat16 or wider, within the bound.
No kernel may reach another device: no remote copies, remote signals or barrier semaphores. Data moves between devices by JAX's collectives and lax.ppermute only.
A program may use at most 64 MiB of HBM per device.

```python
import math
import jax
import jax.numpy as jnp
import numpy as np
from jax import lax

D = 5120
HS = 128
LC = 64
TOK_DEV = 128
TOKENS = 16384
FRAMES = 256
N_SEQ = 128


def draw_score_weights(key, part):
    key = jax.random.fold_in(key, 11)
    base_key = jax.random.fold_in(key, 0)
    scale = LC ** (-0.5)
    base = jnp.clip(jax.random.normal(base_key, (4, 4, LC, D), jnp.float32), -6.0, 6.0)
    return (base * scale).astype(jnp.bfloat16)


def levels(stream_key, shape, pieces, least, high):
    loudness = 1.0
    for dim, parts in pieces:
        draws = jax.random.uniform(jax.random.fold_in(jax.random.fold_in(stream_key, 6), dim), (parts,), jnp.float32, least / len(pieces), high / len(pieces))
        loudness = loudness * jnp.repeat(jnp.exp(draws), shape[dim] // parts).reshape((-1,) + (1,) * (len(shape) - 1 - dim))
    return loudness


def profile(number_of, total, reach, skew):
    weights = [(1 << 20) // math.isqrt(grade ** skew) + 1 for grade in range(2, number_of + 1)]
    rest, counts = total - reach - (number_of - 1), [1] * (number_of - 1)
    while rest > 0:
        candidates = [i for i in range(number_of - 1) if counts[i] < reach]
        mass, left = sum([weights[i] for i in candidates]), rest
        for i in candidates:
            addition = min(reach - counts[i], max(1, left * weights[i] // mass), rest)
            counts[i] = counts[i] + addition
            rest = rest - addition
    return np.array([reach] + counts)


def ragged(rng, count, total, most, slope):
    if count == 2:
        one = jax.random.randint(rng, (), max(1, total - most), min(most, total - 1) + 1)
        return jnp.stack([one, total - one])
    tallies = jnp.asarray(profile(count, total, most, slope), jnp.int32)
    twos = (count - 1) // 2
    giver, sink = tallies[1:1 + 2 * twos:2], tallies[2:2 + 2 * twos:2]
    margin = jnp.minimum(giver - 1, most - sink)
    shifted = jax.random.randint(jax.random.fold_in(rng, 1), (twos,), 0, 1 << 20) % (margin + 1)
    tallies = tallies.at[1:1 + 2 * twos:2].set(giver - shifted).at[2:2 + 2 * twos:2].set(sink + shifted)
    return tallies[jax.random.permutation(jax.random.fold_in(rng, 2), count)]


def centred(rng, shape, width, reach, shards=(), kind=jnp.bfloat16):
    values = width * jax.random.normal(rng, shape, jnp.float32)
    if shards:
        values = values * levels(rng, shape, shards, -0.22, 0.18)
    return jnp.clip(values, -reach, reach).astype(kind)


def setup_inputs(seed: int = 0) -> dict:
    seeds = jax.random.split(jax.random.key(seed), 8)
    return {
        "hidden": centred(seeds[0], (TOKENS, D), 1.0, 6.0, ((0, 128), (1, 4))),
        "gain": jnp.clip(1.0 + 0.15 * jax.random.normal(seeds[1], (D,), jnp.float32), 0.25, 1.75),
        "head_weight": centred(seeds[2], (D, LC), D ** -0.5, 0.078125, ((0, 4),)),
        "noise": centred(seeds[3], (TOKENS, LC), 1.0, 6.0, ((0, 128),)),
        "timestep": jax.random.randint(seeds[4], (1,), 100, 900).astype(jnp.int32),
        "frames": jnp.searchsorted(jnp.cumsum(ragged(seeds[5], FRAMES, TOKENS, TOK_DEV, 1)), jnp.arange(TOKENS), side="right").astype(jnp.int32),
        "score_weights": draw_score_weights(jax.random.fold_in(seeds[7], 71), 0),
    }


DIFF_TABLE = (-3.0, 2.0, 1.5, -0.5)

def frame_mask(frames, first_row, tok_rows):
    padded = jnp.pad(frames, (2 * tok_rows, 2 * tok_rows))
    query_pos = first_row + jnp.arange(tok_rows, dtype=jnp.int32)
    key_pos = first_row - 2 * tok_rows + jnp.arange(4 * tok_rows, dtype=jnp.int32)
    query_frame = lax.dynamic_slice_in_dim(padded, first_row + 2 * tok_rows, tok_rows, 0)
    key_frame = lax.dynamic_slice_in_dim(padded, first_row, 4 * tok_rows, 0)
    inside = (key_pos >= 0) & (key_pos < frames.shape[0])
    return inside[None, :] & (key_frame[None, :] <= query_frame[:, None]) & (query_pos[:, None] - key_pos[None, :] < 2 * tok_rows)

def rounded(values):
    return lax.optimization_barrier(values.astype(jnp.bfloat16)).astype(jnp.float32)

def attend(query, keys, values, visible):
    heads = query.shape[1] // HS
    query_h = query.astype(jnp.float32).reshape(query.shape[0], heads, HS)
    keys_h = keys.astype(jnp.float32).reshape(keys.shape[0], heads, HS)
    values_h = values.astype(jnp.float32).reshape(values.shape[0], heads, HS)
    scores = jnp.einsum('qhd,khd->hqk', query_h, keys_h) * HS ** (-0.5)
    scores = jnp.where(visible[None], scores, -1e+30)
    highest = lax.optimization_barrier(jnp.max(scores, axis=-1, keepdims=True))
    expo = jnp.exp(scores - highest)
    probabilities = expo / lax.optimization_barrier(jnp.sum(expo, axis=-1, keepdims=True))
    attended = jnp.einsum('hqk,khd->qhd', rounded(probabilities), values_h)
    return attended.reshape(query.shape[0], heads * HS).astype(jnp.bfloat16)

def reference(hidden, gain, head_weight, noise, timestep, frames, score_weights):
    hidden_f = hidden.astype(jnp.float32)
    gained = (hidden_f * gain).astype(jnp.bfloat16)
    projected = jnp.dot(gained, head_weight, preferred_element_type=jnp.float32)
    inverse_rms = lax.rsqrt(lax.optimization_barrier(jnp.mean(jnp.square(hidden_f), axis=1)) + 1e-06)
    latent = (inverse_rms[:, None] * projected).astype(jnp.bfloat16)
    phase = 0.5 * math.pi * timestep[0].astype(jnp.float32) / 1000.0
    noisy = (jnp.cos(phase) * latent.astype(jnp.float32) + jnp.sin(phase) * noise.astype(jnp.float32)).astype(jnp.bfloat16)
    padded_noisy = jnp.pad(noisy, ((2 * TOK_DEV, 2 * TOK_DEV), (0, 0)))
    starts = jnp.arange(N_SEQ, dtype=jnp.int32) * TOK_DEV
    score_gap = jnp.zeros((TOKENS, LC), jnp.float32)
    for group in range(4):
        model_weights = score_weights[group]

        def one_block(first_row):
            own_rows = lax.dynamic_slice_in_dim(noisy, first_row, TOK_DEV, 0)
            window_rows = lax.dynamic_slice_in_dim(padded_noisy, first_row, 4 * TOK_DEV, 0)
            query = jnp.dot(own_rows, model_weights[0], preferred_element_type=jnp.float32).astype(jnp.bfloat16)
            keys = jnp.dot(window_rows, model_weights[1], preferred_element_type=jnp.float32).astype(jnp.bfloat16)
            values = jnp.dot(window_rows, model_weights[2], preferred_element_type=jnp.float32).astype(jnp.bfloat16)
            visible = frame_mask(frames, first_row, TOK_DEV)
            attended = attend(query, keys, values, visible)
            return own_rows.astype(jnp.float32) + jnp.dot(attended, model_weights[3].T, preferred_element_type=jnp.float32)
        predicted = lax.map(one_block, starts).reshape(TOKENS, LC)
        score_gap = score_gap + DIFF_TABLE[group] * predicted
    scaled_grad = (inverse_rms[:, None] * score_gap).astype(jnp.bfloat16)
    head_grad = jnp.dot(gained.T, scaled_grad, preferred_element_type=jnp.float32)
    gained_grad = jnp.dot(scaled_grad, head_weight.T, preferred_element_type=jnp.float32)
    gain_grad = lax.optimization_barrier(jnp.sum(hidden_f * gained_grad, axis=0))
    rms_grad = lax.optimization_barrier(jnp.sum(score_gap * projected, axis=1))
    hidden_grad = (gained_grad * gain - (inverse_rms ** 3 * rms_grad / D)[:, None] * hidden_f).astype(jnp.bfloat16)
    return (latent, hidden_grad, head_grad, gain_grad)
```

```python
import functools
import math

import jax
import jax.numpy as jnp
from jax import lax
from jax.experimental import pallas as pl
from jax.experimental.pallas import tpu as pltpu
from jax.sharding import PartitionSpec as P

HS = 128
DIFF_TABLE = (-3.0, 2.0, 1.5, -0.5)
BF = jnp.bfloat16
F32 = jnp.float32
NN = (((1,), (0,)), ((), ()))
NT = (((1,), (1,)), ((), ()))
TN = (((0,), (0,)), ((), ()))
SENT_ROWS = 80
PARAMS = pltpu.CompilerParams(vmem_limit_bytes=40 * 1024 * 1024)


def from_behind(block, axis, distance):
    devices = range(lax.axis_size(axis))
    route = [(i - distance, i) for i in devices if i - distance in devices]
    return lax.ppermute(block, axis, route)


def mm(a, b, dims=NN):
    return lax.dot_general(a, b, dims, preferred_element_type=F32)


def call(body, outs, *args, specs=None, flops=0, scratch=()):
    read = sum(a.size * a.dtype.itemsize for a in args)
    return pl.pallas_call(
        body,
        out_shape=outs,
        in_specs=specs or [pl.BlockSpec(memory_space=pltpu.VMEM)] * len(args),
        scratch_shapes=list(scratch),
        compiler_params=PARAMS,
        cost_estimate=pl.CostEstimate(flops=flops, bytes_accessed=read, transcendentals=0),
    )(*args)


def project_body(hidden_ref, gain_ref, head_ref, out_ref):
    hidden = hidden_ref[...].astype(F32)
    gained = (hidden * gain_ref[...]).astype(BF)
    out_ref[0:64, :] = mm(head_ref[...], gained, NT).astype(BF)
    squares = hidden * hidden
    lanes = functools.reduce(
        jnp.add, [squares[:, i : i + 128] for i in range(0, squares.shape[1], 128)]
    )
    total = jnp.sum(lanes.T, axis=0, keepdims=True)
    high = total.astype(BF).astype(F32)
    row = lax.broadcasted_iota(jnp.int32, (16, 128), 0)
    out_ref[64:80, :] = jnp.where(row == 0, high, jnp.where(row == 1, total - high, 0.0)).astype(BF)


def noisy_body(width, parts_ref, noise_ref, mix_ref, proj_ref, inv_ref, latent_ref, noisy_ref):
    total = jnp.sum(parts_ref[...].astype(F32), axis=0)
    projected = total[0:64]
    inverse = lax.rsqrt((total[64:65] + total[65:66]) / width + 1e-06)
    proj_ref[...] = projected
    inv_ref[...] = inverse
    latent = (inverse * projected).astype(BF)
    latent_ref[...] = latent
    noisy_ref[...] = (
        mix_ref[0] * latent.astype(F32) + mix_ref[1] * noise_ref[...].astype(F32)
    ).astype(BF)


def prepare_body(place_ref, w_ref, frames_ref, hidden_ref, fold_ref, join_ref, bias_ref, spread_ref):
    scale = HS ** (-0.5) * math.log2(math.e)
    heads = w_ref.shape[3] // HS
    zero = jnp.zeros((64, HS), BF)
    for h in range(heads):
        cols = slice(h * HS, (h + 1) * HS)
        fold_ref[h * 64 : (h + 1) * 64, :] = (
            mm(w_ref[0, 1, :, cols], w_ref[0, 0, :, cols], NT) * scale
        ).astype(BF)
    for h in range(0, heads, 2):
        one, two = slice(h * HS, (h + 1) * HS), slice((h + 1) * HS, (h + 2) * HS)
        values = jnp.concatenate(
            [
                jnp.concatenate([w_ref[0, 2, :, one], zero], axis=1),
                jnp.concatenate([zero, w_ref[0, 2, :, two]], axis=1),
            ],
            axis=0,
        )
        join_ref[:, h * 64 : (h + 2) * 64] = mm(
            w_ref[0, 3, :, h * HS : (h + 2) * HS], values, NT
        ).astype(BF)
    place = place_ref[0]
    blocks = frames_ref.shape[0]
    query_frame = frames_ref[pl.ds(place, 1), :]
    ahead = lax.broadcasted_iota(jnp.int32, (128, 128), 0)
    token = lax.broadcasted_iota(jnp.int32, (128, 128), 1)
    for b, offset in enumerate((-2, -1, 0, 1)):
        block = place + offset
        held = jnp.clip(block, 0, blocks - 1)
        key_frame = jnp.broadcast_to(frames_ref[pl.ds(held, 1), :], (128, 128)).T
        key = ahead + offset * 128
        seen = (key_frame <= query_frame) & (token - key < 256)
        seen = seen & (block >= 0) & (block < blocks)
        bias_ref[b * 128 : (b + 1) * 128, :] = jnp.where(seen, 0.0, -1e30).astype(BF)
    features = hidden_ref.shape[1]
    to = lax.broadcasted_iota(jnp.int32, (256, 320), 0)
    source = lax.broadcasted_iota(jnp.int32, (256, 320), 1)
    slot = to & 7
    want = (to >> 3) * 10 + slot
    first = jnp.where((slot < 5) & (source == want), 1.0, 0.0).astype(BF)
    second = jnp.where((slot < 5) & (source == want + 5), 1.0, 0.0).astype(BF)
    for i in range(features // 320):
        piece = hidden_ref[:, i * 320 : (i + 1) * 320]
        rows = slice(i * 256, (i + 1) * 256)
        spread_ref[rows, 0:128] = mm(first, piece, NT).astype(BF)
        spread_ref[rows, 128:256] = mm(second, piece, NT).astype(BF)


def attend_body(
    weight_ref, before2_ref, before1_ref, own_ref, after_ref, fold_ref, join_ref, bias_ref, out_ref,
    query_ref, mixed_ref,
):
    heads = fold_ref.shape[0] // 64
    own = own_ref[...]
    window = jnp.concatenate([before2_ref[...], before1_ref[...], own, after_ref[...]], axis=1)
    row = lax.broadcasted_iota(jnp.int32, (16, 512), 0)
    summing = jnp.concatenate([window, jnp.where(row == 0, 1.0, 0.0).astype(BF)], axis=0)
    keys = jnp.concatenate([window.astype(F32).T.astype(BF), bias_ref[...]], axis=1)
    query_ref[...] = mm(fold_ref[...], own).astype(BF)
    eye = (
        lax.broadcasted_iota(jnp.int32, (128, 128), 0) == lax.broadcasted_iota(jnp.int32, (128, 128), 1)
    )
    eye = jnp.where(eye, 1.0, 0.0).astype(BF)
    eyes = jnp.concatenate([eye, eye], axis=1)
    for h in range(0, heads, 2):
        pair = jnp.concatenate(
            [query_ref[h * 64 : (h + 1) * 64, :], query_ref[(h + 1) * 64 : (h + 2) * 64, :]], axis=1
        )
        scores = mm(keys, jnp.concatenate([pair, eyes], axis=0))
        highest = jnp.max(scores, axis=0, keepdims=True)
        expo = jnp.exp2(scores - highest).astype(BF)
        mixed = mm(summing, expo)
        normal = (mixed[0:64] / mixed[64:65]).astype(BF)
        mixed_ref[h * 64 : (h + 1) * 64, :] = normal[:, 0:128]
        mixed_ref[(h + 1) * 64 : (h + 2) * 64, :] = normal[:, 128:256]
    predicted = own.astype(F32) + mm(join_ref[...], mixed_ref[...])
    out_ref[...] = (weight_ref[0] * predicted).astype(BF)


def gap_body(parts_ref, inv_ref, spread_ref, gap_ref, scaled_ref, terms_ref):
    gap = jnp.sum(parts_ref[...].astype(F32), axis=0)
    gap_ref[...] = gap
    scaled = (inv_ref[...] * gap).astype(BF)
    scaled_ref[...] = scaled
    zero = jnp.zeros_like(scaled)
    both = jnp.concatenate(
        [jnp.concatenate([scaled, zero], axis=1), jnp.concatenate([zero, scaled], axis=1)], axis=0
    )
    terms = mm(spread_ref[...], both, NT)
    terms_ref[...] = terms.reshape(terms_ref.shape).astype(BF)


def hidden_grad_body(
    width, gap_ref, proj_ref, inv_ref, scaled_ref, head_ref, gain_ref, hidden_ref, out_ref
):
    inverse = inv_ref[...]
    rms_grad = jnp.sum(gap_ref[...] * proj_ref[...], axis=0, keepdims=True)
    pull = inverse * inverse * inverse * rms_grad / width
    column = jnp.broadcast_to(pull, (128, 128)).T[:, 0:1]
    gained_grad = mm(scaled_ref[...], head_ref[...], TN)
    out_ref[...] = (
        gained_grad * gain_ref[...] - column * hidden_ref[...].astype(F32)
    ).astype(BF)


def finish_body(terms_ref, gain_ref, head_ref, head_grad_ref, gain_grad_ref):
    total = jnp.sum(terms_ref[...].astype(F32), axis=0)
    rows = jnp.concatenate([total[0:5, 0:64], total[0:5, 64:128]], axis=0)
    head_grad_ref[...] = gain_ref[...] * rows
    gain_grad_ref[...] = jnp.sum(head_ref[...].astype(F32) * rows, axis=1, keepdims=True)


def local(hidden, gain, head_weight, noise, timestep, frames, score_weights):
    shape = jax.ShapeDtypeStruct
    smem, vmem = pl.BlockSpec(memory_space=pltpu.SMEM), pl.BlockSpec(memory_space=pltpu.VMEM)
    tok_rows, features = hidden.shape
    width = features * lax.axis_size("role")
    blocks = lax.axis_size("seq")
    head_t = head_weight.T
    gain_row = gain[None, :]
    place = lax.axis_index("seq").astype(jnp.int32)
    role_index = lax.axis_index("role")
    weighting = jnp.sum(
        jnp.where(jnp.arange(4, dtype=jnp.int32) == role_index, jnp.array(DIFF_TABLE, F32), 0.0)
    )
    phase = 0.5 * math.pi * timestep[0].astype(F32) / 1000.0
    mix = jnp.stack([jnp.cos(phase), jnp.sin(phase)])

    sent = call(project_body, shape((SENT_ROWS, tok_rows), BF), hidden, gain_row, head_t)
    parts = lax.all_gather(sent, "role")
    projected, inverse, latent, noisy = call(
        functools.partial(noisy_body, width),
        (shape((64, tok_rows), F32), shape((1, tok_rows), F32), shape((64, tok_rows), BF), shape((64, tok_rows), BF)),
        parts, noise.T, mix, specs=[vmem, vmem, smem],
    )
    near = [from_behind(noisy, "seq", offset) for offset in (2, 1, -1)]
    fold, join, bias, spread = call(
        prepare_body,
        (shape((2560, 64), BF), shape((64, 2560), BF), shape((512, 128), BF), shape((blocks * 8, 256), BF)),
        place[None], score_weights, frames.reshape(blocks, tok_rows), hidden,
        specs=[smem, vmem, vmem, vmem], flops=2_000_000_000,
    )
    predicted = call(
        attend_body, shape((64, tok_rows), BF),
        weighting[None], near[0], near[1], noisy, near[2], fold, join, bias,
        specs=[smem] + [vmem] * 7, flops=3_000_000_000,
        scratch=[pltpu.VMEM((2560, 128), BF), pltpu.VMEM((2560, 128), BF)],
    )
    gaps = lax.all_gather(predicted, "role")
    gap, scaled, terms = call(
        gap_body,
        (shape((64, tok_rows), F32), shape((64, tok_rows), BF), shape((blocks, 8, 128), BF)),
        gaps, inverse, spread,
    )
    summed = lax.all_to_all(terms, "seq", 0, 0)
    hidden_grad = call(
        functools.partial(hidden_grad_body, width), shape(hidden.shape, BF),
        gap, projected, inverse, scaled, head_t, gain_row, hidden, flops=1_000_000_000,
    )
    own_gain = lax.dynamic_slice_in_dim(gain, place * 10, 10, 0)
    own_head = lax.dynamic_slice_in_dim(head_weight, place * 10, 10, 0)
    head_grad, gain_grad = call(
        finish_body, (shape((10, 64), F32), shape((10, 1), F32)), summed, own_gain[:, None], own_head
    )
    return (latent.T, hidden_grad, head_grad, gain_grad[:, 0])


def solution(mesh):
    in_specs = (
        P("seq", "role"),
        P("role"),
        P("role", None),
        P("seq", None),
        P(),
        P(),
        P("role", None, None, None),
    )
    out_specs = (P("seq", None), P("seq", "role"), P(("role", "seq"), None), P(("role", "seq")))
    return jax.shard_map(local, mesh=mesh, in_specs=in_specs, out_specs=out_specs, check_vma=False)
```

```python
import functools
import math

import jax
import jax.numpy as jnp
from jax import lax
from jax.experimental import pallas as pl
from jax.experimental.pallas import tpu as pltpu
from jax.sharding import PartitionSpec as P

HS = 128
DIFF_TABLE = (-3.0, 2.0, 1.5, -0.5)
BF = jnp.bfloat16
F32 = jnp.float32
NN = (((1,), (0,)), ((), ()))
NT = (((1,), (1,)), ((), ()))
TN = (((0,), (0,)), ((), ()))
SENT_ROWS = 80
GROUP = 4
VMEM, SMEM = pl.BlockSpec(memory_space=pltpu.VMEM), pl.BlockSpec(memory_space=pltpu.SMEM)
HBM = pl.BlockSpec(memory_space=pltpu.HBM)


def from_behind(block, axis, distance):
    devices = range(lax.axis_size(axis))
    route = [(i - distance, i) for i in devices if i - distance in devices]
    return lax.ppermute(block, axis, route)


def mm(a, b, dims=NN):
    return lax.dot_general(a, b, dims, preferred_element_type=F32)


def call(body, outs, *args, specs=None, flops=0, scratch=(), limit=8):
    read = sum(a.size * a.dtype.itemsize for a in args)
    return pl.pallas_call(
        body,
        out_shape=outs,
        in_specs=specs or [VMEM] * len(args),
        scratch_shapes=list(scratch),
        compiler_params=pltpu.CompilerParams(vmem_limit_bytes=limit * 1024 * 1024),
        cost_estimate=pl.CostEstimate(flops=flops, bytes_accessed=read, transcendentals=0),
    )(*args)


def in_hbm(array):
    return pltpu.with_memory_space_constraint(array, pltpu.HBM)


def fetch(pairs, sems):
    copies = [pltpu.make_async_copy(a, b, sems.at[i]) for i, (a, b) in enumerate(pairs)]
    for copy in copies:
        copy.start()
    return copies


def project_body(
    hidden_hbm, gain_hbm, head_hbm, noise_hbm, out_ref, noise_ref, hidden_ref, gain_ref, head_ref,
    sems,
):
    features = hidden_ref.shape[1]
    pieces = [slice(i, i + 256) for i in range(0, features, 256)]
    copies = fetch(
        [(gain_hbm, gain_ref)]
        + [(hidden_hbm.at[:, piece], hidden_ref.at[:, piece]) for piece in pieces]
        + [(head_hbm, head_ref), (noise_hbm, noise_ref)],
        sems,
    )
    copies[0].wait()
    gained, lanes = [], 0.0
    for i in range(features // 128):
        if i % 2 == 0:
            copies[1 + i // 2].wait()
        hidden = hidden_ref[:, i * 128 : (i + 1) * 128].astype(F32)
        gained.append((hidden * gain_ref[i : i + 1, :]).astype(BF))
        lanes = lanes + hidden * hidden
    copies[-2].wait()
    out_ref[0:64, :] = mm(head_ref[...], jnp.concatenate(gained, axis=1), NT).astype(BF)
    total = jnp.sum(lanes.T, axis=0, keepdims=True)
    high = total.astype(BF).astype(F32)
    row = lax.broadcasted_iota(jnp.int32, (16, 128), 0)
    out_ref[64:80, :] = jnp.where(row == 0, high, jnp.where(row == 1, total - high, 0.0)).astype(BF)
    copies[-1].wait()


def noisy_body(width, parts_ref, noise_ref, cos_ref, sin_ref, proj_ref, inv_ref, noisy_ref):
    total = jnp.sum(parts_ref[...].astype(F32), axis=0)
    projected = total[0:64]
    inverse = lax.rsqrt((total[64:65] + total[65:66]) / width + 1e-06)
    proj_ref[...] = projected
    inv_ref[...] = inverse
    latent = (inverse * projected).astype(BF)
    noisy_ref[...] = (
        cos_ref[0] * latent.astype(F32) + sin_ref[0] * noise_ref[...].astype(F32)
    ).astype(BF)


def prepare_body(
    place_ref, w_hbm, frames_hbm, hidden_hbm, fold_ref, join_ref, bias_ref, spread_ref,
    w_ref, frames_ref, hidden_ref, sems,
):
    copies = fetch(
        [
            (frames_hbm, frames_ref),
            (hidden_hbm, hidden_ref),
            (w_hbm.at[0, 0], w_ref.at[0]),
            (w_hbm.at[0, 1], w_ref.at[1]),
            (w_hbm.at[0, 2], w_ref.at[2]),
            (w_hbm.at[0, 3], w_ref.at[3]),
        ],
        sems,
    )
    scale = HS ** (-0.5) * math.log2(math.e)
    heads = w_ref.shape[2] // HS
    zero = jnp.zeros((64, HS), BF)
    place = place_ref[0]
    blocks = frames_ref.shape[0]
    copies[0].wait()
    query_frame = frames_ref[pl.ds(place, 1), :]
    ahead = lax.broadcasted_iota(jnp.int32, (128, 128), 0)
    token = lax.broadcasted_iota(jnp.int32, (128, 128), 1)
    for b, offset in enumerate((-2, -1, 0, 1)):
        block = place + offset
        held = jnp.clip(block, 0, blocks - 1)
        key_frame = jnp.broadcast_to(frames_ref[pl.ds(held, 1), :], (128, 128)).T
        key = ahead + offset * 128
        seen = (key_frame <= query_frame) & (token - key < 256)
        seen = seen & (block >= 0) & (block < blocks)
        bias_ref[b * 128 : (b + 1) * 128, :] = jnp.where(seen, 0.0, -1e30)
    copies[1].wait()
    features = hidden_ref.shape[1]
    to = lax.broadcasted_iota(jnp.int32, (192, 320), 0)
    source = lax.broadcasted_iota(jnp.int32, (192, 320), 1)
    turn = (to * 10923) >> 16
    slot = to - turn * 6
    want = turn * 10 + slot
    first = jnp.where((slot < 5) & (source == want), 1.0, 0.0).astype(BF)
    second = jnp.where((slot < 5) & (source == want + 5), 1.0, 0.0).astype(BF)
    for i in range(features // 320):
        piece = hidden_ref[:, i * 320 : (i + 1) * 320]
        rows = slice(i * 192, (i + 1) * 192)
        spread_ref[rows, 0:128] = mm(first, piece, NT).astype(BF)
        spread_ref[rows, 128:256] = mm(second, piece, NT).astype(BF)
    copies[2].wait()
    copies[3].wait()
    for h in range(heads):
        cols = slice(h * HS, (h + 1) * HS)
        fold_ref[h * 64 : (h + 1) * 64, :] = (
            mm(w_ref[1, :, cols], w_ref[0, :, cols], NT) * scale
        ).astype(BF)
    copies[4].wait()
    copies[5].wait()
    for h in range(0, heads, 2):
        one, two = slice(h * HS, (h + 1) * HS), slice((h + 1) * HS, (h + 2) * HS)
        values = jnp.concatenate(
            [
                jnp.concatenate([w_ref[2, :, one], zero], axis=1),
                jnp.concatenate([zero, w_ref[2, :, two]], axis=1),
            ],
            axis=0,
        )
        join_ref[:, h * 64 : (h + 2) * 64] = mm(
            w_ref[3, :, h * HS : (h + 2) * HS], values, NT
        ).astype(BF)


def attend_body(
    role_ref, before2_ref, before1_ref, own_ref, after_ref, fold_ref, join_ref, bias_ref, out_ref,
    query_ref, mixed_ref,
):
    heads = fold_ref.shape[0] // 64
    own = own_ref[...]
    window = jnp.concatenate([before2_ref[...], before1_ref[...], own, after_ref[...]], axis=1)
    row = lax.broadcasted_iota(jnp.int32, (16, 512), 0)
    summing = jnp.concatenate([window, jnp.where(row == 0, 1.0, 0.0).astype(BF)], axis=0)
    keys = window.astype(F32).T.astype(BF)
    query_ref[...] = mm(fold_ref[...], own).astype(BF)
    bias = jnp.concatenate([bias_ref[...]] * GROUP, axis=1)

    def score(h):
        queries = [query_ref[(h + g) * 64 : (h + g + 1) * 64, :] for g in range(GROUP)]
        return mm(keys, jnp.concatenate(queries, axis=1)) + bias

    def soften(scores):
        return jnp.exp2(scores - jnp.max(scores, axis=0, keepdims=True)).astype(BF)

    def mix(h, expo):
        mixed = mm(summing, expo)
        normal = (mixed[0:64] * (1.0 / mixed[64:65])).astype(BF)
        for g in range(GROUP):
            mixed_ref[(h + g) * 64 : (h + g + 1) * 64, :] = normal[:, g * 128 : (g + 1) * 128]

    scores, expo = score(0), None
    for h in range(0, heads + GROUP, GROUP):
        upcoming = score(h + GROUP) if h + GROUP < heads else None
        current = soften(scores) if h < heads else None
        if expo is not None:
            mix(h - GROUP, expo)
        scores, expo = upcoming, current
    predicted = own.astype(F32) + mm(join_ref[...], mixed_ref[...])
    role = role_ref[0]
    weight = jnp.float32(DIFF_TABLE[0])
    for i in range(1, 4):
        weight = jnp.where(role == i, jnp.float32(DIFF_TABLE[i]), weight)
    out_ref[...] = (weight * predicted).astype(BF)


def gap_body(parts_ref, inv_ref, spread_ref, gap_ref, scaled_ref, terms_ref):
    gap = jnp.sum(parts_ref[...].astype(F32), axis=0)
    gap_ref[...] = gap
    scaled = (inv_ref[...] * gap).astype(BF)
    scaled_ref[...] = scaled
    zero = jnp.zeros_like(scaled)
    both = jnp.concatenate(
        [jnp.concatenate([scaled, zero], axis=1), jnp.concatenate([zero, scaled], axis=1)], axis=0
    )
    terms_ref[...] = mm(spread_ref[...], both, NT).astype(BF)


def hidden_grad_body(
    width, gap_ref, proj_ref, inv_ref, scaled_ref, head_ref, gain_ref, hidden_ref, out_ref,
    latent_ref,
):
    inverse = inv_ref[...]
    projected = proj_ref[...]
    latent_ref[...] = (inverse * projected).astype(BF)
    rms_grad = jnp.sum(gap_ref[...] * projected, axis=0, keepdims=True)
    pull = inverse * inverse * inverse * rms_grad / width
    column = jnp.broadcast_to(pull, (128, 128)).T
    gained_grad = mm(scaled_ref[...], head_ref[...], TN)
    for i in range(hidden_ref.shape[1] // 128):
        cols = slice(i * 128, (i + 1) * 128)
        out_ref[:, cols] = (
            gained_grad[:, cols] * gain_ref[i : i + 1, :] - column * hidden_ref[:, cols].astype(F32)
        ).astype(BF)


def finish_body(terms_ref, gain_ref, head_ref, head_grad_ref, gain_grad_ref):
    total = jnp.sum(terms_ref[...].astype(F32), axis=0)
    rows = jnp.concatenate([total[0:5, 0:64], total[0:5, 64:128]], axis=0)
    head_grad_ref[...] = gain_ref[...] * rows
    column = jnp.sum(head_ref[...].astype(F32) * rows, axis=1, keepdims=True)
    column = jnp.concatenate([column, jnp.zeros((118, 1), F32)], axis=0)
    gain_grad_ref[...] = jnp.broadcast_to(column, (128, 128)).T[0:1, 0:10]


def local(hidden, gain, head_weight, noise, timestep, frames, score_weights):
    shape = jax.ShapeDtypeStruct
    tok_rows, features = hidden.shape
    width = features * lax.axis_size("role")
    blocks = lax.axis_size("seq")
    head_t = head_weight.T
    gain_rows = gain.reshape(features // 128, 128)
    place = lax.axis_index("seq").astype(jnp.int32)
    role = lax.axis_index("role").astype(jnp.int32)
    phase = 0.5 * math.pi * timestep.astype(F32) / 1000.0

    sent, noise_t = call(
        project_body, (shape((SENT_ROWS, tok_rows), BF), shape((64, tok_rows), BF)),
        *map(in_hbm, (hidden, gain_rows, head_t, noise.T)), specs=[HBM] * 4, limit=4,
        scratch=[
            pltpu.VMEM(hidden.shape, BF), pltpu.VMEM(gain_rows.shape, F32),
            pltpu.VMEM(head_t.shape, BF), pltpu.SemaphoreType.DMA((3 + features // 256,)),
        ],
    )
    parts = lax.all_gather(sent, "role")
    projected, inverse, noisy = call(
        functools.partial(noisy_body, width),
        (shape((64, tok_rows), F32), shape((1, tok_rows), F32), shape((64, tok_rows), BF)),
        parts, noise_t, jnp.cos(phase), jnp.sin(phase), specs=[VMEM, VMEM, SMEM, SMEM], limit=2,
    )
    near = [from_behind(noisy, "seq", offset) for offset in (2, 1, -1)]
    fold, join, bias, spread = call(
        prepare_body,
        (
            shape((2560, 64), BF), shape((64, 2560), BF), shape((512, 128), F32),
            shape((blocks * 6, 256), BF),
        ),
        place[None], *map(in_hbm, (score_weights, frames.reshape(blocks, tok_rows), hidden)),
        specs=[SMEM] + [HBM] * 3, flops=2_000_000_000, limit=12,
        scratch=[
            pltpu.VMEM(score_weights.shape[1:], BF), pltpu.VMEM((blocks, tok_rows), jnp.int32),
            pltpu.VMEM(hidden.shape, BF), pltpu.SemaphoreType.DMA((6,)),
        ],
    )
    predicted = call(
        attend_body, shape((64, tok_rows), BF),
        role[None], near[0], near[1], noisy, near[2], fold, join, bias,
        specs=[SMEM] + [VMEM] * 7, flops=3_000_000_000, limit=20,
        scratch=[pltpu.VMEM((2560, 128), BF), pltpu.VMEM((2560, 128), BF)],
    )
    gaps = lax.all_gather(predicted, "role")
    gap, scaled, terms = call(
        gap_body,
        (
            shape((64, tok_rows), F32), shape((64, tok_rows), BF),
            shape((blocks * 6, 128), BF),
        ),
        gaps, inverse, spread,
    )
    summed = lax.all_to_all(terms.reshape(blocks, 3, 2, 128), "seq", 0, 0).reshape(blocks, 6, 128)
    hidden_grad, latent = call(
        functools.partial(hidden_grad_body, width), (shape(hidden.shape, BF), shape((64, tok_rows), BF)),
        gap, projected, inverse, scaled, head_t, gain_rows, hidden, flops=1_000_000_000,
    )
    own_gain = lax.dynamic_slice_in_dim(gain, place * 10, 10, 0)
    own_head = lax.dynamic_slice_in_dim(head_weight, place * 10, 10, 0)
    head_grad, gain_grad = call(
        finish_body, (shape((10, 64), F32), shape((1, 10), F32)), summed, own_gain[:, None], own_head
    )
    return (latent.T, hidden_grad, head_grad, gain_grad[0])


def solution(mesh):
    in_specs = (
        P("seq", "role"),
        P("role"),
        P("role", None),
        P("seq", None),
        P(),
        P(),
        P("role", None, None, None),
    )
    out_specs = (P("seq", None), P("seq", "role"), P(("role", "seq"), None), P(("role", "seq")))
    return jax.shard_map(local, mesh=mesh, in_specs=in_specs, out_specs=out_specs, check_vma=False)
```

```python
import functools
import math

import jax
import jax.numpy as jnp
from jax import lax
from jax.experimental import pallas as pl
from jax.experimental.pallas import tpu as pltpu
from jax.sharding import PartitionSpec as P

HS = 128
DIFF_TABLE = (-3.0, 2.0, 1.5, -0.5)
BF = jnp.bfloat16
F32 = jnp.float32
NN = (((1,), (0,)), ((), ()))
NT = (((1,), (1,)), ((), ()))
TN = (((0,), (0,)), ((), ()))
SENT_ROWS = 80
GROUP = 4
JOIN_FROM = 20
VMEM, SMEM = pl.BlockSpec(memory_space=pltpu.VMEM), pl.BlockSpec(memory_space=pltpu.SMEM)
HBM = pl.BlockSpec(memory_space=pltpu.HBM)


def move(block, target):
    roles, places = lax.axis_size("role"), lax.axis_size("seq")
    route = []
    for r in range(roles):
        for s in range(places):
            to_role, to_place = target(r, s)
            if 0 <= to_place < places:
                route.append((r * places + s, to_role * places + to_place))
    return lax.ppermute(block, ("role", "seq"), route)


def mm(a, b, dims=NN):
    return lax.dot_general(a, b, dims, preferred_element_type=F32)


def call(body, outs, *args, specs=None, flops=0, scratch=(), limit=8):
    read = sum(a.size * a.dtype.itemsize for a in args)
    return pl.pallas_call(
        body,
        out_shape=outs,
        in_specs=specs or [VMEM] * len(args),
        scratch_shapes=list(scratch),
        compiler_params=pltpu.CompilerParams(vmem_limit_bytes=limit * 1024 * 1024),
        cost_estimate=pl.CostEstimate(flops=flops, bytes_accessed=read, transcendentals=0),
    )(*args)


def in_hbm(array):
    return pltpu.with_memory_space_constraint(array, pltpu.HBM)


def fetch(pairs, sems):
    copies = [pltpu.make_async_copy(a, b, sems.at[i]) for i, (a, b) in enumerate(pairs)]
    for copy in copies:
        copy.start()
    return copies


def project_body(
    hidden_hbm, gain_hbm, head_hbm, noise_hbm, frames_hbm, w_hbm, out_ref, noise_ref, hidden_ref,
    frames_ref, w_ref, gain_ref, head_ref, sems,
):
    features = hidden_ref.shape[1]
    pieces = [slice(i, i + 256) for i in range(0, features, 256)]
    copies = fetch(
        [(gain_hbm, gain_ref)]
        + [(hidden_hbm.at[:, piece], hidden_ref.at[:, piece]) for piece in pieces]
        + [(head_hbm, head_ref), (noise_hbm, noise_ref), (frames_hbm, frames_ref)]
        + [(w_hbm.at[0, i], w_ref.at[i]) for i in range(2)],
        sems,
    )
    copies[0].wait()
    gained, lanes = [], 0.0
    for i in range(features // 128):
        if i % 2 == 0:
            copies[1 + i // 2].wait()
        hidden = hidden_ref[:, i * 128 : (i + 1) * 128].astype(F32)
        gained.append((hidden * gain_ref[i : i + 1, :]).astype(BF))
        lanes = lanes + hidden * hidden
    copies[1 + len(pieces)].wait()
    out_ref[0:64, :] = mm(head_ref[...], jnp.concatenate(gained, axis=1), NT).astype(BF)
    total = jnp.sum(lanes.T, axis=0, keepdims=True)
    high = total.astype(BF).astype(F32)
    row = lax.broadcasted_iota(jnp.int32, (16, 128), 0)
    out_ref[64:80, :] = jnp.where(row == 0, high, jnp.where(row == 1, total - high, 0.0)).astype(BF)
    for copy in copies[2 + len(pieces) :]:
        copy.wait()


def noisy_body(width, parts_ref, noise_ref, cos_ref, sin_ref, proj_ref, inv_ref, noisy_ref):
    total = jnp.sum(parts_ref[...].astype(F32), axis=0)
    projected = total[0:64]
    inverse = lax.rsqrt((total[64:65] + total[65:66]) / width + 1e-06)
    proj_ref[...] = projected
    inv_ref[...] = inverse
    latent = (inverse * projected).astype(BF)
    noisy_ref[...] = (
        cos_ref[0] * latent.astype(F32) + sin_ref[0] * noise_ref[...].astype(F32)
    ).astype(BF)


def prepare_body(place_ref, w_ref, frames_ref, hidden_ref, fold_ref, bias_ref, spread_ref):
    scale = HS ** (-0.5) * math.log2(math.e)
    heads = w_ref.shape[2] // HS
    place = place_ref[0]
    blocks = frames_ref.shape[0]
    query_frame = frames_ref[pl.ds(place, 1), :]
    ahead = lax.broadcasted_iota(jnp.int32, (128, 128), 0)
    token = lax.broadcasted_iota(jnp.int32, (128, 128), 1)
    for b, offset in enumerate((-2, -1, 0, 1)):
        block = place + offset
        held = jnp.clip(block, 0, blocks - 1)
        key_frame = jnp.broadcast_to(frames_ref[pl.ds(held, 1), :], (128, 128)).T
        key = ahead + offset * 128
        seen = (key_frame <= query_frame) & (token - key < 256)
        seen = seen & (block >= 0) & (block < blocks)
        bias_ref[b * 128 : (b + 1) * 128, :] = jnp.where(seen, 0.0, -1e30)
    features = hidden_ref.shape[1]
    to = lax.broadcasted_iota(jnp.int32, (192, 320), 0)
    source = lax.broadcasted_iota(jnp.int32, (192, 320), 1)
    turn = (to * 10923) >> 16
    slot = to - turn * 6
    want = turn * 10 + slot
    first = jnp.where((slot < 5) & (source == want), 1.0, 0.0).astype(BF)
    second = jnp.where((slot < 5) & (source == want + 5), 1.0, 0.0).astype(BF)
    for i in range(features // 320):
        piece = hidden_ref[:, i * 320 : (i + 1) * 320]
        rows = slice(i * 192, (i + 1) * 192)
        spread_ref[rows, 0:128] = mm(first, piece, NT).astype(BF)
        spread_ref[rows, 128:256] = mm(second, piece, NT).astype(BF)
    for h in range(heads):
        cols = slice(h * HS, (h + 1) * HS)
        fold_ref[h * 64 : (h + 1) * 64, :] = (
            mm(w_ref[1, :, cols], w_ref[0, :, cols], NT) * scale
        ).astype(BF)


def attend_body(
    role_ref, before1_ref, fetched_ref, swapped_ref, own_ref, fold_ref, bias_ref, w_hbm, out_ref,
    query_ref, mixed_ref, join_ref, w_ref, sems,
):
    values_copy, output_copy = fetch(
        [(w_hbm.at[0, 2], w_ref.at[0]), (w_hbm.at[0, 3], w_ref.at[1])], sems
    )
    heads = fold_ref.shape[0] // 64
    role = role_ref[0]
    own = own_ref[...]
    fetched, swapped = fetched_ref[...], swapped_ref[...]
    first_core = role % 2 == 0
    before2 = jnp.where(first_core, fetched, swapped)
    after = jnp.where(first_core, swapped, fetched)
    window = jnp.concatenate([before2, before1_ref[...], own, after], axis=1)
    row = lax.broadcasted_iota(jnp.int32, (16, 512), 0)
    summing = jnp.concatenate([window, jnp.where(row == 0, 1.0, 0.0).astype(BF)], axis=0)
    keys = window.astype(F32).T.astype(BF)
    query_ref[...] = mm(fold_ref[...], own).astype(BF)
    bias = jnp.concatenate([bias_ref[...]] * GROUP, axis=1)
    zero = jnp.zeros((64, HS), BF)

    def score(h):
        queries = [query_ref[(h + g) * 64 : (h + g + 1) * 64, :] for g in range(GROUP)]
        return mm(keys, jnp.concatenate(queries, axis=1)) + bias

    def soften(scores):
        return jnp.exp2(scores - jnp.max(scores, axis=0, keepdims=True)).astype(BF)

    def mix(h, expo):
        mixed = mm(summing, expo)
        normal = (mixed[0:64] * (1.0 / mixed[64:65])).astype(BF)
        for g in range(GROUP):
            mixed_ref[(h + g) * 64 : (h + g + 1) * 64, :] = normal[:, g * 128 : (g + 1) * 128]

    def join(h):
        one, two = slice(h * HS, (h + 1) * HS), slice((h + 1) * HS, (h + 2) * HS)
        values = jnp.concatenate(
            [
                jnp.concatenate([w_ref[0, :, one], zero], axis=1),
                jnp.concatenate([zero, w_ref[0, :, two]], axis=1),
            ],
            axis=0,
        )
        join_ref[:, h * 64 : (h + 2) * 64] = mm(
            w_ref[1, :, h * HS : (h + 2) * HS], values, NT
        ).astype(BF)

    pairs = list(range(0, heads, 2))
    scores, expo = score(0), None
    for h in range(0, heads + GROUP, GROUP):
        upcoming = score(h + GROUP) if h + GROUP < heads else None
        current = soften(scores) if h < heads else None
        if expo is not None:
            mix(h - GROUP, expo)
        if h == JOIN_FROM:
            values_copy.wait()
            output_copy.wait()
        if h >= JOIN_FROM:
            for _ in range(-(-len(pairs) * GROUP // (heads + GROUP - h))):
                join(pairs.pop(0))
        scores, expo = upcoming, current
    predicted = own.astype(F32) + mm(join_ref[...], mixed_ref[...])
    weight = jnp.float32(DIFF_TABLE[0])
    for i in range(1, 4):
        weight = jnp.where(role == i, jnp.float32(DIFF_TABLE[i]), weight)
    out_ref[...] = (weight * predicted).astype(BF)


def gap_body(parts_ref, inv_ref, spread_ref, gap_ref, scaled_ref, terms_ref):
    gap = jnp.sum(parts_ref[...].astype(F32), axis=0)
    gap_ref[...] = gap
    scaled = (inv_ref[...] * gap).astype(BF)
    scaled_ref[...] = scaled
    zero = jnp.zeros_like(scaled)
    both = jnp.concatenate(
        [jnp.concatenate([scaled, zero], axis=1), jnp.concatenate([zero, scaled], axis=1)], axis=0
    )
    terms_ref[...] = mm(spread_ref[...], both, NT).astype(BF)


def hidden_grad_body(
    width, gap_ref, proj_ref, inv_ref, scaled_ref, head_ref, gain_ref, hidden_ref, out_ref,
    latent_ref,
):
    inverse = inv_ref[...]
    projected = proj_ref[...]
    latent_ref[...] = (inverse * projected).astype(BF)
    rms_grad = jnp.sum(gap_ref[...] * projected, axis=0, keepdims=True)
    pull = inverse * inverse * inverse * rms_grad / width
    column = jnp.broadcast_to(pull, (128, 128)).T
    gained_grad = mm(scaled_ref[...], head_ref[...], TN)
    for i in range(hidden_ref.shape[1] // 128):
        cols = slice(i * 128, (i + 1) * 128)
        out_ref[:, cols] = (
            gained_grad[:, cols] * gain_ref[i : i + 1, :] - column * hidden_ref[:, cols].astype(F32)
        ).astype(BF)


def finish_body(terms_ref, gain_ref, head_ref, head_grad_ref, gain_grad_ref):
    total = jnp.sum(terms_ref[...].astype(F32), axis=0)
    rows = jnp.concatenate([total[0:5, 0:64], total[0:5, 64:128]], axis=0)
    head_grad_ref[...] = gain_ref[...] * rows
    column = jnp.sum(head_ref[...].astype(F32) * rows, axis=1, keepdims=True)
    column = jnp.concatenate([column, jnp.zeros((118, 1), F32)], axis=0)
    gain_grad_ref[...] = jnp.broadcast_to(column, (128, 128)).T[0:1, 0:10]


def local(hidden, gain, head_weight, noise, timestep, frames, score_weights):
    shape = jax.ShapeDtypeStruct
    tok_rows, features = hidden.shape
    width = features * lax.axis_size("role")
    blocks = lax.axis_size("seq")
    head_t = head_weight.T
    gain_rows = gain.reshape(features // 128, 128)
    place = lax.axis_index("seq").astype(jnp.int32)
    role = lax.axis_index("role").astype(jnp.int32)
    phase = 0.5 * math.pi * timestep.astype(F32) / 1000.0

    wide = score_weights.shape[2:]
    sent, noise_t, hidden_v, frames_v, query_key = call(
        project_body,
        (
            shape((SENT_ROWS, tok_rows), BF), shape((64, tok_rows), BF), shape(hidden.shape, BF),
            shape((blocks, tok_rows), jnp.int32), shape((2, *wide), BF),
        ),
        *map(
            in_hbm,
            (
                hidden, gain_rows, head_t, noise.T, frames.reshape(blocks, tok_rows),
                score_weights,
            ),
        ),
        specs=[HBM] * 6,
        scratch=[
            pltpu.VMEM(gain_rows.shape, F32), pltpu.VMEM(head_t.shape, BF),
            pltpu.SemaphoreType.DMA((6 + features // 256,)),
        ],
    )
    parts = lax.all_gather(sent, "role")
    projected, inverse, noisy = call(
        functools.partial(noisy_body, width),
        (shape((64, tok_rows), F32), shape((1, tok_rows), F32), shape((64, tok_rows), BF)),
        parts, noise_t, jnp.cos(phase), jnp.sin(phase), specs=[VMEM, VMEM, SMEM, SMEM], limit=2,
    )
    fetched = move(noisy, lambda r, s: (r, s + 2 if r % 2 == 0 else s - 1))
    before1 = move(noisy, lambda r, s: (r, s + 1))
    swapped = move(fetched, lambda r, s: (r ^ 1, s))
    fold, bias, spread = call(
        prepare_body,
        (shape((2560, 64), BF), shape((512, 128), F32), shape((blocks * 6, 256), BF)),
        place[None], query_key, frames_v, hidden_v, specs=[SMEM] + [VMEM] * 3,
        flops=2_000_000_000,
    )
    predicted = call(
        attend_body, shape((64, tok_rows), BF),
        role[None], before1, fetched, swapped, noisy, fold, bias, in_hbm(score_weights),
        specs=[SMEM] + [VMEM] * 6 + [HBM], flops=3_000_000_000, limit=24,
        scratch=[
            pltpu.VMEM((2560, 128), BF), pltpu.VMEM((2560, 128), BF), pltpu.VMEM((64, 2560), BF),
            pltpu.VMEM((2, *wide), BF), pltpu.SemaphoreType.DMA((2,)),
        ],
    )
    gaps = lax.all_gather(predicted, "role")
    gap, scaled, terms = call(
        gap_body,
        (
            shape((64, tok_rows), F32), shape((64, tok_rows), BF),
            shape((blocks * 6, 128), BF),
        ),
        gaps, inverse, spread,
    )
    summed = lax.all_to_all(terms.reshape(blocks, 3, 2, 128), "seq", 0, 0).reshape(blocks, 6, 128)
    hidden_grad, latent = call(
        functools.partial(hidden_grad_body, width), (shape(hidden.shape, BF), shape((64, tok_rows), BF)),
        gap, projected, inverse, scaled, head_t, gain_rows, hidden_v, flops=1_000_000_000,
    )
    own_gain = lax.dynamic_slice_in_dim(gain, place * 10, 10, 0)
    own_head = lax.dynamic_slice_in_dim(head_weight, place * 10, 10, 0)
    head_grad, gain_grad = call(
        finish_body, (shape((10, 64), F32), shape((1, 10), F32)), summed, own_gain[:, None], own_head
    )
    return (latent.T, hidden_grad, head_grad, gain_grad[0])


def solution(mesh):
    in_specs = (
        P("seq", "role"),
        P("role"),
        P("role", None),
        P("seq", None),
        P(),
        P(),
        P("role", None, None, None),
    )
    out_specs = (P("seq", None), P("seq", "role"), P(("role", "seq"), None), P(("role", "seq")))
    return jax.shard_map(local, mesh=mesh, in_specs=in_specs, out_specs=out_specs, check_vma=False)
```

```python
import functools
import math

import jax
import jax.numpy as jnp
from jax import lax
from jax.experimental import pallas as pl
from jax.experimental.pallas import tpu as pltpu
from jax.sharding import PartitionSpec as P

HS = 128
DIFF_TABLE = (-3.0, 2.0, 1.5, -0.5)
BF = jnp.bfloat16
F32 = jnp.float32
NN = (((1,), (0,)), ((), ()))
NT = (((1,), (1,)), ((), ()))
TN = (((0,), (0,)), ((), ()))
HINT = 8_000_000_000
SENT_ROWS = 80
GROUP = 4
JOIN_FROM = 20
VMEM, SMEM = pl.BlockSpec(memory_space=pltpu.VMEM), pl.BlockSpec(memory_space=pltpu.SMEM)
HBM = pl.BlockSpec(memory_space=pltpu.HBM)


def move(block, target):
    roles, places = lax.axis_size("role"), lax.axis_size("seq")
    route = []
    for r in range(roles):
        for s in range(places):
            to_role, to_place = target(r, s)
            if 0 <= to_place < places:
                route.append((r * places + s, to_role * places + to_place))
    return lax.ppermute(block, ("role", "seq"), route)


def mm(a, b, dims=NN):
    return lax.dot_general(a, b, dims, preferred_element_type=F32)


def call(body, outs, *args, specs=None, flops=0, scratch=(), limit=8):
    read = sum(a.size * a.dtype.itemsize for a in args)
    return pl.pallas_call(
        body,
        out_shape=outs,
        in_specs=specs or [VMEM] * len(args),
        scratch_shapes=list(scratch),
        compiler_params=pltpu.CompilerParams(vmem_limit_bytes=limit * 1024 * 1024),
        cost_estimate=pl.CostEstimate(flops=flops, bytes_accessed=read, transcendentals=0),
    )(*args)


def in_hbm(array):
    return pltpu.with_memory_space_constraint(array, pltpu.HBM)


def fetch(pairs, sems):
    copies = [pltpu.make_async_copy(a, b, sems.at[i]) for i, (a, b) in enumerate(pairs)]
    for copy in copies:
        copy.start()
    return copies


def project_body(
    hidden_hbm, gain_hbm, head_hbm, noise_hbm, frames_hbm, out_ref, noise_ref, hidden_ref,
    frames_ref, gain_ref, head_ref, sems,
):
    features = hidden_ref.shape[1]
    pieces = [slice(i, i + 256) for i in range(0, features, 256)]
    copies = fetch(
        [(gain_hbm, gain_ref)]
        + [(hidden_hbm.at[:, piece], hidden_ref.at[:, piece]) for piece in pieces]
        + [(head_hbm, head_ref), (noise_hbm, noise_ref), (frames_hbm, frames_ref)],
        sems,
    )
    copies[0].wait()
    gained, lanes = [], 0.0
    for i in range(features // 128):
        if i % 2 == 0:
            copies[1 + i // 2].wait()
        hidden = hidden_ref[:, i * 128 : (i + 1) * 128].astype(F32)
        gained.append((hidden * gain_ref[i : i + 1, :]).astype(BF))
        lanes = lanes + hidden * hidden
    copies[1 + len(pieces)].wait()
    out_ref[0:64, :] = mm(head_ref[...], jnp.concatenate(gained, axis=1), NT).astype(BF)
    total = jnp.sum(lanes.T, axis=0, keepdims=True)
    high = total.astype(BF).astype(F32)
    row = lax.broadcasted_iota(jnp.int32, (16, 128), 0)
    out_ref[64:80, :] = jnp.where(row == 0, high, jnp.where(row == 1, total - high, 0.0)).astype(BF)
    for copy in copies[2 + len(pieces) :]:
        copy.wait()


def noisy_body(width, parts_ref, noise_ref, cos_ref, sin_ref, proj_ref, inv_ref, noisy_ref):
    total = jnp.sum(parts_ref[...].astype(F32), axis=0)
    projected = total[0:64]
    inverse = lax.rsqrt((total[64:65] + total[65:66]) / width + 1e-06)
    proj_ref[...] = projected
    inv_ref[...] = inverse
    latent = (inverse * projected).astype(BF)
    noisy_ref[...] = (
        cos_ref[0] * latent.astype(F32) + sin_ref[0] * noise_ref[...].astype(F32)
    ).astype(BF)


def prepare_body(place_ref, w_ref, frames_ref, hidden_ref, fold_ref, bias_ref, spread_ref):
    scale = HS ** (-0.5) * math.log2(math.e)
    heads = w_ref.shape[3] // HS
    place = place_ref[0]
    blocks = frames_ref.shape[0]
    query_frame = frames_ref[pl.ds(place, 1), :]
    ahead = lax.broadcasted_iota(jnp.int32, (128, 128), 0)
    token = lax.broadcasted_iota(jnp.int32, (128, 128), 1)
    for b, offset in enumerate((-2, -1, 0, 1)):
        block = place + offset
        held = jnp.clip(block, 0, blocks - 1)
        key_frame = jnp.broadcast_to(frames_ref[pl.ds(held, 1), :], (128, 128)).T
        key = ahead + offset * 128
        seen = (key_frame <= query_frame) & (token - key < 256)
        seen = seen & (block >= 0) & (block < blocks)
        bias_ref[b * 128 : (b + 1) * 128, :] = jnp.where(seen, 0.0, -1e30)
    features = hidden_ref.shape[1]
    to = lax.broadcasted_iota(jnp.int32, (192, 320), 0)
    source = lax.broadcasted_iota(jnp.int32, (192, 320), 1)
    turn = (to * 10923) >> 16
    slot = to - turn * 6
    want = turn * 10 + slot
    first = jnp.where((slot < 5) & (source == want), 1.0, 0.0).astype(BF)
    second = jnp.where((slot < 5) & (source == want + 5), 1.0, 0.0).astype(BF)
    for i in range(features // 320):
        piece = hidden_ref[:, i * 320 : (i + 1) * 320]
        rows = slice(i * 192, (i + 1) * 192)
        spread_ref[rows, 0:128] = mm(first, piece, NT).astype(BF)
        spread_ref[rows, 128:256] = mm(second, piece, NT).astype(BF)
    for h in range(heads):
        cols = slice(h * HS, (h + 1) * HS)
        fold_ref[h * 64 : (h + 1) * 64, :] = (
            mm(w_ref[0, 1, :, cols], w_ref[0, 0, :, cols], NT) * scale
        ).astype(BF)


def attend_body(
    role_ref, before1_ref, fetched_ref, swapped_ref, own_ref, fold_ref, bias_ref, w_ref, out_ref,
    query_ref, mixed_ref, join_ref,
):
    heads = fold_ref.shape[0] // 64
    role = role_ref[0]
    own = own_ref[...]
    fetched, swapped = fetched_ref[...], swapped_ref[...]
    first_core = role % 2 == 0
    before2 = jnp.where(first_core, fetched, swapped)
    after = jnp.where(first_core, swapped, fetched)
    window = jnp.concatenate([before2, before1_ref[...], own, after], axis=1)
    row = lax.broadcasted_iota(jnp.int32, (16, 512), 0)
    summing = jnp.concatenate([window, jnp.where(row == 0, 1.0, 0.0).astype(BF)], axis=0)
    keys = window.astype(F32).T.astype(BF)
    query_ref[...] = mm(fold_ref[...], own).astype(BF)
    bias = jnp.concatenate([bias_ref[...]] * GROUP, axis=1)
    zero = jnp.zeros((64, HS), BF)

    def score(h):
        queries = [query_ref[(h + g) * 64 : (h + g + 1) * 64, :] for g in range(GROUP)]
        return mm(keys, jnp.concatenate(queries, axis=1)) + bias

    def soften(scores):
        return jnp.exp2(scores - jnp.max(scores, axis=0, keepdims=True)).astype(BF)

    def mix(h, expo):
        mixed = mm(summing, expo)
        normal = (mixed[0:64] * (1.0 / mixed[64:65])).astype(BF)
        for g in range(GROUP):
            mixed_ref[(h + g) * 64 : (h + g + 1) * 64, :] = normal[:, g * 128 : (g + 1) * 128]

    def join(h):
        one, two = slice(h * HS, (h + 1) * HS), slice((h + 1) * HS, (h + 2) * HS)
        values = jnp.concatenate(
            [
                jnp.concatenate([w_ref[0, 2, :, one], zero], axis=1),
                jnp.concatenate([zero, w_ref[0, 2, :, two]], axis=1),
            ],
            axis=0,
        )
        join_ref[:, h * 64 : (h + 2) * 64] = mm(
            w_ref[0, 3, :, h * HS : (h + 2) * HS], values, NT
        ).astype(BF)

    pairs = list(range(0, heads, 2))
    scores, expo = score(0), None
    for h in range(0, heads + GROUP, GROUP):
        upcoming = score(h + GROUP) if h + GROUP < heads else None
        current = soften(scores) if h < heads else None
        if expo is not None:
            mix(h - GROUP, expo)
        if h >= JOIN_FROM:
            for _ in range(-(-len(pairs) * GROUP // (heads + GROUP - h))):
                join(pairs.pop(0))
        scores, expo = upcoming, current
    predicted = own.astype(F32) + mm(join_ref[...], mixed_ref[...])
    weight = jnp.float32(DIFF_TABLE[0])
    for i in range(1, 4):
        weight = jnp.where(role == i, jnp.float32(DIFF_TABLE[i]), weight)
    out_ref[...] = (weight * predicted).astype(BF)


def gap_body(parts_ref, inv_ref, spread_ref, gap_ref, scaled_ref, terms_ref):
    gap = jnp.sum(parts_ref[...].astype(F32), axis=0)
    gap_ref[...] = gap
    scaled = (inv_ref[...] * gap).astype(BF)
    scaled_ref[...] = scaled
    zero = jnp.zeros_like(scaled)
    both = jnp.concatenate(
        [jnp.concatenate([scaled, zero], axis=1), jnp.concatenate([zero, scaled], axis=1)], axis=0
    )
    terms_ref[...] = mm(spread_ref[...], both, NT).astype(BF)


def hidden_grad_body(
    width, gap_ref, proj_ref, inv_ref, scaled_ref, head_ref, gain_ref, hidden_ref, out_ref,
    latent_ref,
):
    inverse = inv_ref[...]
    projected = proj_ref[...]
    latent_ref[...] = (inverse * projected).astype(BF)
    rms_grad = jnp.sum(gap_ref[...] * projected, axis=0, keepdims=True)
    pull = inverse * inverse * inverse * rms_grad / width
    column = jnp.broadcast_to(pull, (128, 128)).T
    gained_grad = mm(scaled_ref[...], head_ref[...], TN)
    for i in range(hidden_ref.shape[1] // 128):
        cols = slice(i * 128, (i + 1) * 128)
        out_ref[:, cols] = (
            gained_grad[:, cols] * gain_ref[i : i + 1, :] - column * hidden_ref[:, cols].astype(F32)
        ).astype(BF)


def finish_body(terms_ref, gain_ref, head_ref, head_grad_ref, gain_grad_ref):
    total = jnp.sum(terms_ref[...].astype(F32).reshape(-1, 24, 128), axis=0)
    total = total[0:6] + total[6:12] + total[12:18] + total[18:24]
    rows = jnp.concatenate([total[0:5, 0:64], total[0:5, 64:128]], axis=0)
    head_grad_ref[...] = gain_ref[...] * rows
    column = jnp.sum(head_ref[...].astype(F32) * rows, axis=1, keepdims=True)
    column = jnp.concatenate([column, jnp.zeros((118, 1), F32)], axis=0)
    gain_grad_ref[...] = jnp.broadcast_to(column, (128, 128)).T[0:1, 0:10]


def local(hidden, gain, head_weight, noise, timestep, frames, score_weights):
    shape = jax.ShapeDtypeStruct
    tok_rows, features = hidden.shape
    width = features * lax.axis_size("role")
    blocks = lax.axis_size("seq")
    head_t = head_weight.T
    gain_rows = gain.reshape(features // 128, 128)
    place = lax.axis_index("seq").astype(jnp.int32)
    role = lax.axis_index("role").astype(jnp.int32)
    phase = 0.5 * math.pi * timestep.astype(F32) / 1000.0

    sent, noise_t, hidden_v, frames_v = call(
        project_body,
        (
            shape((SENT_ROWS, tok_rows), BF), shape((64, tok_rows), BF), shape(hidden.shape, BF),
            shape((blocks, tok_rows), jnp.int32),
        ),
        *map(
            in_hbm,
            (hidden, gain_rows, head_t, noise.T, frames.reshape(blocks, tok_rows)),
        ),
        specs=[HBM] * 5,
        scratch=[
            pltpu.VMEM(gain_rows.shape, F32), pltpu.VMEM(head_t.shape, BF),
            pltpu.SemaphoreType.DMA((4 + features // 256,)),
        ],
    )
    parts = lax.all_gather(sent, "role")
    projected, inverse, noisy = call(
        functools.partial(noisy_body, width),
        (shape((64, tok_rows), F32), shape((1, tok_rows), F32), shape((64, tok_rows), BF)),
        parts, noise_t, jnp.cos(phase), jnp.sin(phase), specs=[VMEM, VMEM, SMEM, SMEM], limit=2,
        flops=HINT,
    )
    fetched = move(noisy, lambda r, s: (r, s + 2 if r % 2 == 0 else s - 1))
    before1 = move(noisy, lambda r, s: (r, s + 1))
    swapped = move(fetched, lambda r, s: (r ^ 1, s))
    fold, bias, spread = call(
        prepare_body,
        (shape((2560, 64), BF), shape((512, 128), F32), shape((blocks * 6, 256), BF)),
        place[None], score_weights, frames_v, hidden_v, specs=[SMEM] + [VMEM] * 3,
        flops=1_000_000,
    )
    predicted = call(
        attend_body, shape((64, tok_rows), BF),
        role[None], before1, fetched, swapped, noisy, fold, bias, score_weights,
        specs=[SMEM] + [VMEM] * 7, flops=3_000_000_000, limit=24,
        scratch=[
            pltpu.VMEM((2560, 128), BF), pltpu.VMEM((2560, 128), BF), pltpu.VMEM((64, 2560), BF),
        ],
    )
    gaps = lax.all_gather(predicted, "role")
    gap, scaled, terms = call(
        gap_body,
        (
            shape((64, tok_rows), F32), shape((64, tok_rows), BF),
            shape((blocks * 6, 128), BF),
        ),
        gaps, inverse, spread,
    )
    summed = lax.all_to_all(terms.reshape(blocks, 3, 2, 128), "seq", 0, 0).reshape(blocks * 6, 128)
    hidden_grad, latent = call(
        functools.partial(hidden_grad_body, width), (shape(hidden.shape, BF), shape((64, tok_rows), BF)),
        gap, projected, inverse, scaled, head_t, gain_rows, hidden_v, flops=1_000_000_000,
    )
    own_gain = lax.dynamic_slice_in_dim(gain, place * 10, 10, 0)
    own_head = lax.dynamic_slice_in_dim(head_weight, place * 10, 10, 0)
    head_grad, gain_grad = call(
        finish_body, (shape((10, 64), F32), shape((1, 10), F32)), summed, own_gain[:, None], own_head
    )
    return (latent.T, hidden_grad, head_grad, gain_grad[0])


def solution(mesh):
    in_specs = (
        P("seq", "role"),
        P("role"),
        P("role", None),
        P("seq", None),
        P(),
        P(),
        P("role", None, None, None),
    )
    out_specs = (P("seq", None), P("seq", "role"), P(("role", "seq"), None), P(("role", "seq")))
    return jax.shard_map(local, mesh=mesh, in_specs=in_specs, out_specs=out_specs, check_vma=False)
```

```python
import functools
import math

import jax
import jax.numpy as jnp
from jax import lax
from jax.experimental import pallas as pl
from jax.experimental.pallas import tpu as pltpu
from jax.sharding import PartitionSpec as P

HS = 128
DIFF_TABLE = (-3.0, 2.0, 1.5, -0.5)
BF = jnp.bfloat16
F32 = jnp.float32
NN = (((1,), (0,)), ((), ()))
NT = (((1,), (1,)), ((), ()))
TN = (((0,), (0,)), ((), ()))
HINT = 8_000_000_000
SENT_ROWS = 80
GROUP = 4
VMEM, SMEM = pl.BlockSpec(memory_space=pltpu.VMEM), pl.BlockSpec(memory_space=pltpu.SMEM)
HBM = pl.BlockSpec(memory_space=pltpu.HBM)


def move(block, target):
    roles, places = lax.axis_size("role"), lax.axis_size("seq")
    route = []
    for r in range(roles):
        for s in range(places):
            to_role, to_place = target(r, s)
            if 0 <= to_place < places:
                route.append((r * places + s, to_role * places + to_place))
    return lax.ppermute(block, ("role", "seq"), route)


def mm(a, b, dims=NN):
    return lax.dot_general(a, b, dims, preferred_element_type=F32)


def call(body, outs, *args, specs=None, flops=0, scratch=(), limit=8):
    read = sum(a.size * a.dtype.itemsize for a in args)
    return pl.pallas_call(
        body,
        out_shape=outs,
        in_specs=specs or [VMEM] * len(args),
        scratch_shapes=list(scratch),
        compiler_params=pltpu.CompilerParams(vmem_limit_bytes=limit * 1024 * 1024),
        cost_estimate=pl.CostEstimate(flops=flops, bytes_accessed=read, transcendentals=0),
    )(*args)


def in_hbm(array):
    return pltpu.with_memory_space_constraint(array, pltpu.HBM)


def fetch(pairs, sems):
    copies = [pltpu.make_async_copy(a, b, sems.at[i]) for i, (a, b) in enumerate(pairs)]
    for copy in copies:
        copy.start()
    return copies


def project_body(
    hidden_hbm, gain_hbm, head_hbm, noise_hbm, frames_hbm, out_ref, noise_ref, hidden_ref,
    frames_ref, gain_ref, head_ref, sems,
):
    features = hidden_ref.shape[1]
    pieces = [slice(i, i + 256) for i in range(0, features, 256)]
    copies = fetch(
        [(gain_hbm, gain_ref)]
        + [(hidden_hbm.at[:, piece], hidden_ref.at[:, piece]) for piece in pieces]
        + [(head_hbm, head_ref), (noise_hbm, noise_ref), (frames_hbm, frames_ref)],
        sems,
    )
    copies[0].wait()
    gained, lanes = [], 0.0
    for i in range(features // 128):
        if i % 2 == 0:
            copies[1 + i // 2].wait()
        hidden = hidden_ref[:, i * 128 : (i + 1) * 128].astype(F32)
        gained.append((hidden * gain_ref[i : i + 1, :]).astype(BF))
        lanes = lanes + hidden * hidden
    copies[1 + len(pieces)].wait()
    out_ref[0:64, :] = mm(head_ref[...], jnp.concatenate(gained, axis=1), NT).astype(BF)
    total = jnp.sum(lanes.T, axis=0, keepdims=True)
    high = total.astype(BF).astype(F32)
    row = lax.broadcasted_iota(jnp.int32, (16, 128), 0)
    out_ref[64:80, :] = jnp.where(row == 0, high, jnp.where(row == 1, total - high, 0.0)).astype(BF)
    for copy in copies[2 + len(pieces) :]:
        copy.wait()


def noisy_body(width, parts_ref, noise_ref, cos_ref, sin_ref, proj_ref, inv_ref, noisy_ref):
    total = jnp.sum(parts_ref[...].astype(F32), axis=0)
    projected = total[0:64]
    inverse = lax.rsqrt((total[64:65] + total[65:66]) / width + 1e-06)
    proj_ref[...] = projected
    inv_ref[...] = inverse
    latent = (inverse * projected).astype(BF)
    noisy_ref[...] = (
        cos_ref[0] * latent.astype(F32) + sin_ref[0] * noise_ref[...].astype(F32)
    ).astype(BF)


def prepare_body(place_ref, w_ref, frames_ref, hidden_ref, fold_ref, bias_ref, spread_ref):
    scale = HS ** (-0.5) * math.log2(math.e)
    heads = w_ref.shape[3] // HS
    place = place_ref[0]
    blocks = frames_ref.shape[0]
    query_frame = frames_ref[pl.ds(place, 1), :]
    ahead = lax.broadcasted_iota(jnp.int32, (128, 128), 0)
    token = lax.broadcasted_iota(jnp.int32, (128, 128), 1)
    for b, offset in enumerate((-2, -1, 0, 1)):
        block = place + offset
        held = jnp.clip(block, 0, blocks - 1)
        key_frame = jnp.broadcast_to(frames_ref[pl.ds(held, 1), :], (128, 128)).T
        key = ahead + offset * 128
        seen = (key_frame <= query_frame) & (token - key < 256)
        seen = seen & (block >= 0) & (block < blocks)
        bias_ref[b * 128 : (b + 1) * 128, :] = jnp.where(seen, 0.0, -1e30)
    features = hidden_ref.shape[1]
    to = lax.broadcasted_iota(jnp.int32, (192, 320), 0)
    source = lax.broadcasted_iota(jnp.int32, (192, 320), 1)
    turn = (to * 10923) >> 16
    slot = to - turn * 6
    want = turn * 10 + slot
    first = jnp.where((slot < 5) & (source == want), 1.0, 0.0).astype(BF)
    second = jnp.where((slot < 5) & (source == want + 5), 1.0, 0.0).astype(BF)
    for i in range(features // 320):
        piece = hidden_ref[:, i * 320 : (i + 1) * 320]
        rows = slice(i * 192, (i + 1) * 192)
        spread_ref[rows, 0:128] = mm(first, piece, NT).astype(BF)
        spread_ref[rows, 128:256] = mm(second, piece, NT).astype(BF)
    for h in range(heads):
        cols = slice(h * HS, (h + 1) * HS)
        fold_ref[h * 64 : (h + 1) * 64, :] = (
            mm(w_ref[0, 1, :, cols], w_ref[0, 0, :, cols], NT) * scale
        ).astype(BF)


def attend_body(
    role_ref, before1_ref, fetched_ref, swapped_ref, own_ref, fold_ref, bias_ref, w_ref, out_ref,
    query_ref, mixed_ref, join_ref,
):
    heads = fold_ref.shape[0] // 64
    role = role_ref[0]
    own = own_ref[...]
    fetched, swapped = fetched_ref[...], swapped_ref[...]
    first_core = role % 2 == 0
    before2 = jnp.where(first_core, fetched, swapped)
    after = jnp.where(first_core, swapped, fetched)
    window = jnp.concatenate([before2, before1_ref[...], own, after], axis=1)
    row = lax.broadcasted_iota(jnp.int32, (16, 512), 0)
    summing = jnp.concatenate([window, jnp.where(row == 0, 1.0, 0.0).astype(BF)], axis=0)
    keys = window.astype(F32).T.astype(BF)
    query_ref[...] = mm(fold_ref[...], own).astype(BF)
    bias = jnp.concatenate([bias_ref[...]] * GROUP, axis=1)
    zero = jnp.zeros((64, HS), BF)

    def score(h):
        queries = [query_ref[(h + g) * 64 : (h + g + 1) * 64, :] for g in range(GROUP)]
        return mm(keys, jnp.concatenate(queries, axis=1)) + bias

    def soften(scores):
        return jnp.exp2(scores - jnp.max(scores, axis=0, keepdims=True)).astype(BF)

    def mix(h, expo):
        mixed = mm(summing, expo)
        normal = (mixed[0:64] * (1.0 / mixed[64:65])).astype(BF)
        for g in range(GROUP):
            mixed_ref[(h + g) * 64 : (h + g + 1) * 64, :] = normal[:, g * 128 : (g + 1) * 128]

    def join(h):
        one, two = slice(h * HS, (h + 1) * HS), slice((h + 1) * HS, (h + 2) * HS)
        values = jnp.concatenate(
            [
                jnp.concatenate([w_ref[0, 2, :, one], zero], axis=1),
                jnp.concatenate([zero, w_ref[0, 2, :, two]], axis=1),
            ],
            axis=0,
        )
        join_ref[:, h * 64 : (h + 2) * 64] = mm(
            w_ref[0, 3, :, h * HS : (h + 2) * HS], values, NT
        ).astype(BF)

    pairs = list(range(0, heads, 2))
    scores, expo = score(0), None
    for h in range(0, heads + GROUP, GROUP):
        upcoming = score(h + GROUP) if h + GROUP < heads else None
        current = soften(scores) if h < heads else None
        if expo is not None:
            mix(h - GROUP, expo)
        for _ in range(-(-len(pairs) * GROUP // (heads + GROUP - h))):
            join(pairs.pop(0))
        scores, expo = upcoming, current
    predicted = own.astype(F32) + mm(join_ref[...], mixed_ref[...])
    weight = jnp.float32(DIFF_TABLE[0])
    for i in range(1, 4):
        weight = jnp.where(role == i, jnp.float32(DIFF_TABLE[i]), weight)
    out_ref[...] = (weight * predicted).astype(BF)


def gap_body(parts_ref, inv_ref, spread_ref, gap_ref, scaled_ref, terms_ref):
    gap = jnp.sum(parts_ref[...].astype(F32), axis=0)
    gap_ref[...] = gap
    scaled = (inv_ref[...] * gap).astype(BF)
    scaled_ref[...] = scaled
    zero = jnp.zeros_like(scaled)
    both = jnp.concatenate(
        [jnp.concatenate([scaled, zero], axis=1), jnp.concatenate([zero, scaled], axis=1)], axis=0
    )
    terms_ref[...] = mm(spread_ref[...], both, NT).astype(BF)


def hidden_grad_body(
    width, gap_ref, proj_ref, inv_ref, scaled_ref, head_ref, gain_ref, hidden_ref, out_ref,
    latent_ref,
):
    inverse = inv_ref[...]
    projected = proj_ref[...]
    latent_ref[...] = (inverse * projected).astype(BF)
    rms_grad = jnp.sum(gap_ref[...] * projected, axis=0, keepdims=True)
    pull = inverse * inverse * inverse * rms_grad / width
    column = jnp.broadcast_to(pull, (128, 128)).T
    gained_grad = mm(scaled_ref[...], head_ref[...], TN)
    for i in range(hidden_ref.shape[1] // 128):
        cols = slice(i * 128, (i + 1) * 128)
        out_ref[:, cols] = (
            gained_grad[:, cols] * gain_ref[i : i + 1, :] - column * hidden_ref[:, cols].astype(F32)
        ).astype(BF)


def finish_body(terms_ref, gain_ref, head_ref, head_grad_ref, gain_grad_ref):
    total = jnp.sum(terms_ref[...].astype(F32).reshape(-1, 24, 128), axis=0)
    total = total[0:6] + total[6:12] + total[12:18] + total[18:24]
    rows = jnp.concatenate([total[0:5, 0:64], total[0:5, 64:128]], axis=0)
    head_grad_ref[...] = gain_ref[...] * rows
    column = jnp.sum(head_ref[...].astype(F32) * rows, axis=1, keepdims=True)
    column = jnp.concatenate([column, jnp.zeros((118, 1), F32)], axis=0)
    gain_grad_ref[...] = jnp.broadcast_to(column, (128, 128)).T[0:1, 0:10]


def local(hidden, gain, head_weight, noise, timestep, frames, score_weights):
    shape = jax.ShapeDtypeStruct
    tok_rows, features = hidden.shape
    width = features * lax.axis_size("role")
    blocks = lax.axis_size("seq")
    head_t = head_weight.T
    gain_rows = gain.reshape(features // 128, 128)
    place = lax.axis_index("seq").astype(jnp.int32)
    role = lax.axis_index("role").astype(jnp.int32)
    phase = 0.5 * math.pi * timestep.astype(F32) / 1000.0

    sent, noise_t, hidden_v, frames_v = call(
        project_body,
        (
            shape((SENT_ROWS, tok_rows), BF), shape((64, tok_rows), BF), shape(hidden.shape, BF),
            shape((blocks, tok_rows), jnp.int32),
        ),
        *map(
            in_hbm,
            (hidden, gain_rows, head_t, noise.T, frames.reshape(blocks, tok_rows)),
        ),
        specs=[HBM] * 5,
        scratch=[
            pltpu.VMEM(gain_rows.shape, F32), pltpu.VMEM(head_t.shape, BF),
            pltpu.SemaphoreType.DMA((4 + features // 256,)),
        ],
    )
    parts = lax.all_gather(sent, "role")
    projected, inverse, noisy = call(
        functools.partial(noisy_body, width),
        (shape((64, tok_rows), F32), shape((1, tok_rows), F32), shape((64, tok_rows), BF)),
        parts, noise_t, jnp.cos(phase), jnp.sin(phase), specs=[VMEM, VMEM, SMEM, SMEM], limit=2,
        flops=HINT,
    )
    fetched = move(noisy, lambda r, s: (r, s + 2 if r % 2 == 0 else s - 1))
    before1 = move(noisy, lambda r, s: (r, s + 1))
    swapped = move(fetched, lambda r, s: (r ^ 1, s))
    fold, bias, spread = call(
        prepare_body,
        (shape((2560, 64), BF), shape((512, 128), F32), shape((blocks * 6, 256), BF)),
        place[None], score_weights, frames_v, hidden_v, specs=[SMEM] + [VMEM] * 3,
        flops=1_000_000,
    )
    predicted = call(
        attend_body, shape((64, tok_rows), BF),
        role[None], before1, fetched, swapped, noisy, fold, bias, score_weights,
        specs=[SMEM] + [VMEM] * 7, flops=3_000_000_000, limit=24,
        scratch=[
            pltpu.VMEM((2560, 128), BF), pltpu.VMEM((2560, 128), BF), pltpu.VMEM((64, 2560), BF),
        ],
    )
    gaps = lax.all_gather(predicted, "role")
    gap, scaled, terms = call(
        gap_body,
        (
            shape((64, tok_rows), F32), shape((64, tok_rows), BF),
            shape((blocks * 6, 128), BF),
        ),
        gaps, inverse, spread,
    )
    summed = lax.all_to_all(terms.reshape(blocks, 3, 2, 128), "seq", 0, 0).reshape(blocks * 6, 128)
    hidden_grad, latent = call(
        functools.partial(hidden_grad_body, width), (shape(hidden.shape, BF), shape((64, tok_rows), BF)),
        gap, projected, inverse, scaled, head_t, gain_rows, hidden_v, flops=1_000_000_000,
    )
    own_gain = lax.dynamic_slice_in_dim(gain, place * 10, 10, 0)
    own_head = lax.dynamic_slice_in_dim(head_weight, place * 10, 10, 0)
    head_grad, gain_grad = call(
        finish_body, (shape((10, 64), F32), shape((1, 10), F32)), summed, own_gain[:, None], own_head
    )
    return (latent.T, hidden_grad, head_grad, gain_grad[0])


def solution(mesh):
    in_specs = (
        P("seq", "role"),
        P("role"),
        P("role", None),
        P("seq", None),
        P(),
        P(),
        P("role", None, None, None),
    )
    out_specs = (P("seq", None), P("seq", "role"), P(("role", "seq"), None), P(("role", "seq")))
    return jax.shard_map(local, mesh=mesh, in_specs=in_specs, out_specs=out_specs, check_vma=False)
```

```python
import functools
import math

import jax
import jax.numpy as jnp
from jax import lax
from jax.experimental import pallas as pl
from jax.experimental.pallas import tpu as pltpu
from jax.sharding import PartitionSpec as P

HS = 128
DIFF_TABLE = (-3.0, 2.0, 1.5, -0.5)
BF = jnp.bfloat16
F32 = jnp.float32
NN = (((1,), (0,)), ((), ()))
NT = (((1,), (1,)), ((), ()))
TN = (((0,), (0,)), ((), ()))
HINT = 8_000_000_000
SENT_ROWS = 80
GROUP = 4
VMEM, SMEM = pl.BlockSpec(memory_space=pltpu.VMEM), pl.BlockSpec(memory_space=pltpu.SMEM)
HBM = pl.BlockSpec(memory_space=pltpu.HBM)


def move(block, target):
    roles, places = lax.axis_size("role"), lax.axis_size("seq")
    route = []
    for r in range(roles):
        for s in range(places):
            to_role, to_place = target(r, s)
            if 0 <= to_place < places:
                route.append((r * places + s, to_role * places + to_place))
    return lax.ppermute(block, ("role", "seq"), route)


def mm(a, b, dims=NN):
    return lax.dot_general(a, b, dims, preferred_element_type=F32)


def call(body, outs, *args, specs=None, flops=0, scratch=(), limit=8):
    read = sum(a.size * a.dtype.itemsize for a in args)
    return pl.pallas_call(
        body,
        out_shape=outs,
        in_specs=specs or [VMEM] * len(args),
        scratch_shapes=list(scratch),
        compiler_params=pltpu.CompilerParams(vmem_limit_bytes=limit * 1024 * 1024),
        cost_estimate=pl.CostEstimate(flops=flops, bytes_accessed=read, transcendentals=0),
    )(*args)


def in_hbm(array):
    return pltpu.with_memory_space_constraint(array, pltpu.HBM)


def fetch(pairs, sems):
    copies = [pltpu.make_async_copy(a, b, sems.at[i]) for i, (a, b) in enumerate(pairs)]
    for copy in copies:
        copy.start()
    return copies


def project_body(
    hidden_hbm, gain_hbm, head_hbm, noise_hbm, frames_hbm, out_ref, noise_ref, hidden_ref,
    frames_ref, gain_ref, head_ref, sems,
):
    features = hidden_ref.shape[1]
    pieces = [slice(i, i + 256) for i in range(0, features, 256)]
    copies = fetch(
        [(gain_hbm, gain_ref), (head_hbm, head_ref)]
        + [(hidden_hbm.at[:, piece], hidden_ref.at[:, piece]) for piece in pieces]
        + [(noise_hbm, noise_ref), (frames_hbm, frames_ref)],
        sems,
    )
    copies[0].wait()
    copies[1].wait()
    projected, lanes = 0.0, 0.0
    for copy, piece in zip(copies[2:], pieces):
        copy.wait()
        gained = []
        for i in range(piece.start // 128, piece.stop // 128):
            hidden = hidden_ref[:, i * 128 : (i + 1) * 128].astype(F32)
            gained.append((hidden * gain_ref[i : i + 1, :]).astype(BF))
            lanes = lanes + hidden * hidden
        projected = projected + mm(head_ref[:, piece], jnp.concatenate(gained, axis=1), NT)
    out_ref[0:64, :] = projected.astype(BF)
    total = jnp.sum(lanes.T, axis=0, keepdims=True)
    high = total.astype(BF).astype(F32)
    row = lax.broadcasted_iota(jnp.int32, (16, 128), 0)
    out_ref[64:80, :] = jnp.where(row == 0, high, jnp.where(row == 1, total - high, 0.0)).astype(BF)
    for copy in copies[2 + len(pieces) :]:
        copy.wait()


def noisy_body(width, parts_ref, noise_ref, cos_ref, sin_ref, proj_ref, inv_ref, noisy_ref):
    total = jnp.sum(parts_ref[...].astype(F32), axis=0)
    projected = total[0:64]
    inverse = lax.rsqrt((total[64:65] + total[65:66]) / width + 1e-06)
    proj_ref[...] = projected
    inv_ref[...] = inverse
    latent = (inverse * projected).astype(BF)
    noisy_ref[...] = (
        cos_ref[0] * latent.astype(F32) + sin_ref[0] * noise_ref[...].astype(F32)
    ).astype(BF)


def prepare_body(place_ref, w_ref, frames_ref, hidden_ref, fold_ref, bias_ref, spread_ref):
    scale = HS ** (-0.5) * math.log2(math.e)
    heads = w_ref.shape[3] // HS
    place = place_ref[0]
    blocks = frames_ref.shape[0]
    query_frame = frames_ref[pl.ds(place, 1), :]
    ahead = lax.broadcasted_iota(jnp.int32, (128, 128), 0)
    token = lax.broadcasted_iota(jnp.int32, (128, 128), 1)
    for b, offset in enumerate((-2, -1, 0, 1)):
        block = place + offset
        held = jnp.clip(block, 0, blocks - 1)
        key_frame = jnp.broadcast_to(frames_ref[pl.ds(held, 1), :], (128, 128)).T
        key = ahead + offset * 128
        seen = (key_frame <= query_frame) & (token - key < 256)
        seen = seen & (block >= 0) & (block < blocks)
        bias_ref[b * 128 : (b + 1) * 128, :] = jnp.where(seen, 0.0, -1e30)
    features = hidden_ref.shape[1]
    to = lax.broadcasted_iota(jnp.int32, (192, 320), 0)
    source = lax.broadcasted_iota(jnp.int32, (192, 320), 1)
    turn = (to * 10923) >> 16
    slot = to - turn * 6
    want = turn * 10 + slot
    first = jnp.where((slot < 5) & (source == want), 1.0, 0.0).astype(BF)
    second = jnp.where((slot < 5) & (source == want + 5), 1.0, 0.0).astype(BF)
    for i in range(features // 320):
        piece = hidden_ref[:, i * 320 : (i + 1) * 320]
        rows = slice(i * 192, (i + 1) * 192)
        spread_ref[rows, 0:128] = mm(first, piece, NT).astype(BF)
        spread_ref[rows, 128:256] = mm(second, piece, NT).astype(BF)
    for h in range(heads):
        cols = slice(h * HS, (h + 1) * HS)
        fold_ref[h * 64 : (h + 1) * 64, :] = (
            mm(w_ref[0, 1, :, cols], w_ref[0, 0, :, cols], NT) * scale
        ).astype(BF)


def attend_body(
    role_ref, before1_ref, fetched_ref, swapped_ref, own_ref, fold_ref, bias_ref, w_ref, out_ref,
    query_ref, mixed_ref, join_ref,
):
    heads = fold_ref.shape[0] // 64
    role = role_ref[0]
    own = own_ref[...]
    fetched, swapped = fetched_ref[...], swapped_ref[...]
    first_core = role % 2 == 0
    before2 = jnp.where(first_core, fetched, swapped)
    after = jnp.where(first_core, swapped, fetched)
    window = jnp.concatenate([before2, before1_ref[...], own, after], axis=1)
    row = lax.broadcasted_iota(jnp.int32, (16, 512), 0)
    summing = jnp.concatenate([window, jnp.where(row == 0, 1.0, 0.0).astype(BF)], axis=0)
    keys = window.astype(F32).T.astype(BF)
    query_ref[...] = mm(fold_ref[...], own).astype(BF)
    bias = jnp.concatenate([bias_ref[...]] * GROUP, axis=1)
    zero = jnp.zeros((64, HS), BF)

    def score(h):
        queries = [query_ref[(h + g) * 64 : (h + g + 1) * 64, :] for g in range(GROUP)]
        return mm(keys, jnp.concatenate(queries, axis=1)) + bias

    def soften(scores):
        return jnp.exp2(scores - jnp.max(scores, axis=0, keepdims=True)).astype(BF)

    def mix(h, expo):
        mixed = mm(summing, expo)
        normal = (mixed[0:64] * (1.0 / mixed[64:65])).astype(BF)
        for g in range(GROUP):
            mixed_ref[(h + g) * 64 : (h + g + 1) * 64, :] = normal[:, g * 128 : (g + 1) * 128]

    def join(h):
        one, two = slice(h * HS, (h + 1) * HS), slice((h + 1) * HS, (h + 2) * HS)
        values = jnp.concatenate(
            [
                jnp.concatenate([w_ref[0, 2, :, one], zero], axis=1),
                jnp.concatenate([zero, w_ref[0, 2, :, two]], axis=1),
            ],
            axis=0,
        )
        join_ref[:, h * 64 : (h + 2) * 64] = mm(
            w_ref[0, 3, :, h * HS : (h + 2) * HS], values, NT
        ).astype(BF)

    pairs = list(range(0, heads, 2))
    scores, expo = score(0), None
    for h in range(0, heads + GROUP, GROUP):
        upcoming = score(h + GROUP) if h + GROUP < heads else None
        current = soften(scores) if h < heads else None
        if expo is not None:
            mix(h - GROUP, expo)
        for _ in range(-(-len(pairs) * GROUP // (heads + GROUP - h))):
            join(pairs.pop(0))
        scores, expo = upcoming, current
    predicted = own.astype(F32) + mm(join_ref[...], mixed_ref[...])
    weight = jnp.float32(DIFF_TABLE[0])
    for i in range(1, 4):
        weight = jnp.where(role == i, jnp.float32(DIFF_TABLE[i]), weight)
    out_ref[...] = (weight * predicted).astype(BF)


def gap_body(parts_ref, inv_ref, spread_ref, gap_ref, scaled_ref, terms_ref):
    gap = jnp.sum(parts_ref[...].astype(F32), axis=0)
    gap_ref[...] = gap
    scaled = (inv_ref[...] * gap).astype(BF)
    scaled_ref[...] = scaled
    zero = jnp.zeros_like(scaled)
    both = jnp.concatenate(
        [jnp.concatenate([scaled, zero], axis=1), jnp.concatenate([zero, scaled], axis=1)], axis=0
    )
    terms_ref[...] = mm(spread_ref[...], both, NT).astype(BF)


def hidden_grad_body(
    width, gap_ref, proj_ref, inv_ref, scaled_ref, head_ref, gain_ref, hidden_ref, out_ref,
    latent_ref,
):
    inverse = inv_ref[...]
    projected = proj_ref[...]
    latent_ref[...] = (inverse * projected).astype(BF)
    rms_grad = jnp.sum(gap_ref[...] * projected, axis=0, keepdims=True)
    pull = inverse * inverse * inverse * rms_grad / width
    column = jnp.broadcast_to(pull, (128, 128)).T
    gained_grad = mm(scaled_ref[...], head_ref[...], TN)
    for i in range(hidden_ref.shape[1] // 128):
        cols = slice(i * 128, (i + 1) * 128)
        out_ref[:, cols] = (
            gained_grad[:, cols] * gain_ref[i : i + 1, :] - column * hidden_ref[:, cols].astype(F32)
        ).astype(BF)


def finish_body(terms_ref, gain_ref, head_ref, head_grad_ref, gain_grad_ref):
    total = jnp.sum(terms_ref[...].astype(F32).reshape(-1, 24, 128), axis=0)
    total = total[0:6] + total[6:12] + total[12:18] + total[18:24]
    rows = jnp.concatenate([total[0:5, 0:64], total[0:5, 64:128]], axis=0)
    head_grad_ref[...] = gain_ref[...] * rows
    column = jnp.sum(head_ref[...].astype(F32) * rows, axis=1, keepdims=True)
    column = jnp.concatenate([column, jnp.zeros((118, 1), F32)], axis=0)
    gain_grad_ref[...] = jnp.broadcast_to(column, (128, 128)).T[0:1, 0:10]


def local(hidden, gain, head_weight, noise, timestep, frames, score_weights):
    shape = jax.ShapeDtypeStruct
    tok_rows, features = hidden.shape
    width = features * lax.axis_size("role")
    blocks = lax.axis_size("seq")
    head_t = head_weight.T
    gain_rows = gain.reshape(features // 128, 128)
    place = lax.axis_index("seq").astype(jnp.int32)
    role = lax.axis_index("role").astype(jnp.int32)
    phase = 0.5 * math.pi * timestep.astype(F32) / 1000.0

    sent, noise_t, hidden_v, frames_v = call(
        project_body,
        (
            shape((SENT_ROWS, tok_rows), BF), shape((64, tok_rows), BF), shape(hidden.shape, BF),
            shape((blocks, tok_rows), jnp.int32),
        ),
        *map(
            in_hbm,
            (hidden, gain_rows, head_t, noise.T, frames.reshape(blocks, tok_rows)),
        ),
        specs=[HBM] * 5,
        scratch=[
            pltpu.VMEM(gain_rows.shape, F32), pltpu.VMEM(head_t.shape, BF),
            pltpu.SemaphoreType.DMA((4 + features // 256,)),
        ],
    )
    parts = lax.all_gather(sent, "role")
    projected, inverse, noisy = call(
        functools.partial(noisy_body, width),
        (shape((64, tok_rows), F32), shape((1, tok_rows), F32), shape((64, tok_rows), BF)),
        parts, noise_t, jnp.cos(phase), jnp.sin(phase), specs=[VMEM, VMEM, SMEM, SMEM], limit=2,
        flops=HINT,
    )
    fetched = move(noisy, lambda r, s: (r, s + 2 if r % 2 == 0 else s - 1))
    before1 = move(noisy, lambda r, s: (r, s + 1))
    swapped = move(fetched, lambda r, s: (r ^ 1, s))
    fold, bias, spread = call(
        prepare_body,
        (shape((2560, 64), BF), shape((512, 128), F32), shape((blocks * 6, 256), BF)),
        place[None], score_weights, frames_v, hidden_v, specs=[SMEM] + [VMEM] * 3,
        flops=1_000_000,
    )
    predicted = call(
        attend_body, shape((64, tok_rows), BF),
        role[None], before1, fetched, swapped, noisy, fold, bias, score_weights,
        specs=[SMEM] + [VMEM] * 7, flops=3_000_000_000, limit=24,
        scratch=[
            pltpu.VMEM((2560, 128), BF), pltpu.VMEM((2560, 128), BF), pltpu.VMEM((64, 2560), BF),
        ],
    )
    gaps = lax.all_gather(predicted, "role")
    gap, scaled, terms = call(
        gap_body,
        (
            shape((64, tok_rows), F32), shape((64, tok_rows), BF),
            shape((blocks * 6, 128), BF),
        ),
        gaps, inverse, spread,
    )
    summed = lax.all_to_all(terms.reshape(blocks, 3, 2, 128), "seq", 0, 0).reshape(blocks * 6, 128)
    hidden_grad, latent = call(
        functools.partial(hidden_grad_body, width), (shape(hidden.shape, BF), shape((64, tok_rows), BF)),
        gap, projected, inverse, scaled, head_t, gain_rows, hidden_v, flops=1_000_000_000,
    )
    own_gain = lax.dynamic_slice_in_dim(gain, place * 10, 10, 0)
    own_head = lax.dynamic_slice_in_dim(head_weight, place * 10, 10, 0)
    head_grad, gain_grad = call(
        finish_body, (shape((10, 64), F32), shape((1, 10), F32)), summed, own_gain[:, None], own_head
    )
    return (latent.T, hidden_grad, head_grad, gain_grad[0])


def solution(mesh):
    in_specs = (
        P("seq", "role"),
        P("role"),
        P("role", None),
        P("seq", None),
        P(),
        P(),
        P("role", None, None, None),
    )
    out_specs = (P("seq", None), P("seq", "role"), P(("role", "seq"), None), P(("role", "seq")))
    return jax.shard_map(local, mesh=mesh, in_specs=in_specs, out_specs=out_specs, check_vma=False)
```
